256 devices in a mesh: depth: 32 (over x, y, core), tile: 8 (over z).
Axes of the slice: x: 4, y: 4, z: 8, core: 2. Of those that a mesh axis runs over, the one named last changes fastest.
Arguments:
- fronts: float32 [32, 8, 8, 2, 128, 128], P('depth', 'tile'), may hold values from -6 to 6
- probe_wave: float32 [2, 128, 128], replicated, may hold values from -6 to 6
- object_slices: bfloat16 [64, 2, 3072, 384], P('depth', None, 'tile')
- patch_list: int32 [35, 8, 3, 8], P(None, 'tile'), may hold values from 0 to 256, as said below
- counts: int32 [35, 8], P(None, 'tile'), may hold values from 1 to 8, as said below
Outputs:
- exit_waves: float32 [32, 8, 8, 2, 128, 128], P('depth', 'tile')
The draws below stay inside these ranges and needn't reach their ends.
Inputs may be any that keep to these rules, and one draw needn't show every extreme that they name: `patch_list`: rows and columns of corners run from 0 to 256, and that end is reached. Among the live probes of one batch of one owner no tile is named more than 1 times; a batch of 8 probes names every tile exactly 1 times. `counts`: some batch of some owner holds 8 probes.
All inputs are finite; a program needn't handle non-finite values.
Results may differ from the reference program's by a relative error of at most 0.0003.
Values may be sent and summed in bfloat16 or wider, within the bound.
A program may use at most 64 MiB of HBM per device.

```python
import math
import jax
import jax.numpy as jnp
from jax import lax

W = 128
TSIDE = 384
SLOTS = 8
STEPS = 4
SLICES = 64
BATCHES = 35
REGION = 3072
N_DEPTH = 32
N_TILE = 8


def draw_object_slices(key, part):
    shape = (SLICES, REGION, TSIDE)
    first_key = jax.random.fold_in(key, 31)
    second_key = jax.random.fold_in(key, 32)
    amplitude = jax.random.uniform(first_key, shape, jnp.float32, 0.8, 1.0)
    phase = jax.random.uniform(second_key, shape, jnp.float32, -math.pi, math.pi)
    return jnp.stack([amplitude * jnp.cos(phase), amplitude * jnp.sin(phase)], axis=1).astype(jnp.bfloat16)


def draw_counts(key, part):
    upper = max(2, 2 * SLOTS // 3)
    base = jax.random.randint(jax.random.fold_in(key, 11), (BATCHES * N_TILE,), 1, upper + 1, dtype=jnp.int32)
    location = jax.random.randint(jax.random.fold_in(key, 12), (), 0, BATCHES * N_TILE, dtype=jnp.int32)
    base = base.at[location].set(SLOTS)
    return base.reshape(BATCHES, N_TILE)


def draw_patch_list(key, part):
    pair = SLOTS // N_TILE
    keys = jax.random.split(jax.random.fold_in(key, 21), BATCHES * N_TILE)
    orders = jax.vmap(lambda one: jax.random.permutation(one, SLOTS))(keys).astype(jnp.int32)
    tile_ids = (orders // pair).reshape(BATCHES, N_TILE, SLOTS)
    row_start = jax.random.randint(jax.random.fold_in(key, 22), (BATCHES * N_TILE * SLOTS,), 0, TSIDE - W + 1, dtype=jnp.int32)
    location = jax.random.randint(jax.random.fold_in(key, 23), (), 0, BATCHES * N_TILE * SLOTS, dtype=jnp.int32)
    row_start = row_start.at[location].set(TSIDE - W).reshape(BATCHES, N_TILE, SLOTS)
    column_start = jax.random.randint(jax.random.fold_in(key, 24), (BATCHES, N_TILE, SLOTS), 0, TSIDE - W + 1, dtype=jnp.int32)
    return jnp.stack([tile_ids, row_start, column_start], axis=2)


def level_of(rng, extent, cuts, low, largest):
    def one(position, parts):
        draws = jax.random.uniform(jax.random.fold_in(jax.random.fold_in(rng, 6), position), (parts,), jnp.float32, low / len(cuts), largest / len(cuts))
        return jnp.repeat(jnp.exp(draws), extent[position] // parts).reshape((-1,) + (1,) * (len(extent) - position - 1))

    factor_of = one(*cuts[0])
    for cut in cuts[1:]:
        factor_of = factor_of * one(*cut)
    return factor_of


def noise(stream_key, extent, scale, limit, cuts=(), held_as=jnp.bfloat16):
    drawn = jax.random.normal(stream_key, extent, jnp.float32) * scale
    if len(cuts) > 0:
        drawn = level_of(stream_key, extent, cuts, -0.22, 0.18) * drawn
    return jnp.clip(drawn, min=-limit, max=limit).astype(held_as)


def setup_inputs(seed: int = 0) -> dict:
    splits = jax.random.split(jax.random.key(seed), 6)
    fronts = noise(splits[0], (N_DEPTH, N_TILE, SLOTS, 2, W, W), 1.0, 6.0, ((0, 32), (1, 8)), jnp.float32)
    probe_wave = noise(splits[1], (2, W, W), 1.0, 6.0, (), jnp.float32)
    object_slices = draw_object_slices(jax.random.fold_in(splits[5], 71), 0)
    patch_list = draw_patch_list(jax.random.fold_in(splits[5], 71), 0)
    counts = draw_counts(jax.random.fold_in(splits[5], 71), 0)
    return {"fronts": fronts, "probe_wave": probe_wave, "object_slices": object_slices, "patch_list": patch_list, "counts": counts}


fresnel_rate = 0.3


def dft_tables(width, inverse):
    index = jnp.arange(width, dtype=jnp.int32)
    angle = (2.0 * math.pi / width) * ((index[:, None] * index[None, :]) % width).astype(jnp.float32)
    cosine = jnp.cos(angle)
    sine = jnp.sin(angle)
    if inverse:
        cosine = cosine / width
        imagine = sine / width
    else:
        imagine = -sine
    return (cosine, cosine + imagine, imagine - cosine)


def plane_dot(plane, table):
    shape = plane.shape
    flat = plane.reshape(-1, shape[-1])
    return jnp.dot(flat, table, precision=lax.Precision.HIGHEST, preferred_element_type=jnp.float32).reshape(shape)


def right_multiply(real_part, imag_part, tables):
    cosine, summed, differ = tables
    first = plane_dot(real_part + imag_part, cosine)
    second = plane_dot(real_part, differ)
    third = plane_dot(imag_part, summed)
    return first - third, first + second


def transform(real_part, imag_part, tables):
    real_part, imag_part = right_multiply(real_part, imag_part, tables)
    return right_multiply(jnp.swapaxes(real_part, -1, -2), jnp.swapaxes(imag_part, -1, -2), tables)


def fresnel(width):
    index = jnp.arange(width, dtype=jnp.int32)
    freq = jnp.where(index < width // 2, index, index - width).astype(jnp.float32)
    phase = (-2.0 * math.pi * fresnel_rate / width) * (freq[:, None] ** 2 + freq[None, :] ** 2)
    return jnp.cos(phase), jnp.sin(phase)


def slab_pass(wavefield, patches):
    width = wavefield.shape[-1]
    forward = dft_tables(width, False)
    backward = dft_tables(width, True)
    kernel_cos, kernel_sin = fresnel(width)
    real_part = wavefield[:, 0]
    imag_part = wavefield[:, 1]
    for layer in range(2):
        trans_real = patches[:, layer, 0].astype(jnp.float32)
        trans_imag = patches[:, layer, 1].astype(jnp.float32)
        real_part, imag_part = real_part * trans_real - imag_part * trans_imag, real_part * trans_imag + imag_part * trans_real
        spec_real, spec_imag = transform(real_part, imag_part, forward)
        spec_real, spec_imag = spec_real * kernel_cos - spec_imag * kernel_sin, spec_real * kernel_sin + spec_imag * kernel_cos
        real_part, imag_part = transform(spec_real, spec_imag, backward)
    return jnp.stack([real_part, imag_part], axis=1)


def reference(fronts, probe_wave, object_slices, patch_list, counts):
    slot_index = jnp.arange(SLOTS, dtype=jnp.int32)

    def one_slab(depth_index):
        batch = (N_DEPTH + STEPS - 2 - depth_index).astype(jnp.int32)
        listing = lax.dynamic_index_in_dim(patch_list, batch, 0, keepdims=False)
        count_row = lax.dynamic_index_in_dim(counts, batch, 0, keepdims=False)
        live = (slot_index[None, :] < count_row[:, None]).astype(jnp.float32)
        source = jnp.maximum(depth_index - STEPS + 1, 0).astype(jnp.int32)
        held = lax.dynamic_index_in_dim(fronts, source, 0, keepdims=False)
        start = jnp.where(depth_index >= STEPS - 1, held, probe_wave[None, None]) * live[:, :, None, None, None]
        wavefield = start.reshape(N_TILE * SLOTS, 2, W, W)
        row_start = (listing[:, 0] * TSIDE + listing[:, 1]).reshape(-1).astype(jnp.int32)
        column_start = listing[:, 2].reshape(-1).astype(jnp.int32)
        for section in range(STEPS):
            slab = depth_index - STEPS + 1 + section
            layers = lax.dynamic_slice_in_dim(object_slices, (2 * jnp.maximum(slab, 0)).astype(jnp.int32), 2, 0)

            def cut_patch(row_value, column_value):
                zero = jnp.zeros((), jnp.int32)
                return lax.dynamic_slice(layers, (zero, zero, row_value, column_value), (2, 2, W, W))

            patches = jax.vmap(cut_patch)(row_start, column_start)
            moved = slab_pass(wavefield, patches)
            wavefield = jnp.where(slab >= 0, moved, wavefield)
        return wavefield.reshape(N_TILE, SLOTS, 2, W, W)

    return lax.map(one_slab, jnp.arange(N_DEPTH, dtype=jnp.int32))
```

```python
import functools
import math

import jax
import jax.numpy as jnp
import ml_dtypes
import numpy as np
from jax import lax
from jax.experimental import pallas as pl
from jax.experimental.pallas import tpu as pltpu
from jax.sharding import PartitionSpec as P

STEPS = 4
FRESNEL_RATE = 0.3
MESH = pl.DeviceIdType.MESH

ROWS = 272
TOP = 32766.0


def split_table(table):
    high = table.astype(ml_dtypes.bfloat16)
    low = (table - high.astype(np.float64)).astype(ml_dtypes.bfloat16)
    return high, low


def propagator(width):
    index = np.arange(width)
    angle = 2.0 * math.pi / width * ((index[:, None] * index[None, :]) % width)
    forward = np.cos(angle) - 1j * np.sin(angle)
    inverse = (np.cos(angle) + 1j * np.sin(angle)) / width
    freq = np.where(index < width // 2, index, index - width).astype(np.float64)
    phase = -2.0 * math.pi * FRESNEL_RATE / width * freq**2
    matrix = inverse @ ((np.cos(phase) + 1j * np.sin(phase))[:, None] * forward)
    real, imag = matrix.real, matrix.imag
    right = np.block([[real, imag], [-imag, real]])
    left = np.block([[real, -imag], [imag, real]])
    return split_table(right) + split_table(left)


def offset_of(slot):
    return lax.rem(8 + (lax.rem(slot, 2) * 2 - 1) * ((slot + 1) // 2), 8)


def encode(plane):
    groups = plane.reshape(16, 8, 128)
    largest = jnp.maximum(jnp.max(jnp.abs(groups), axis=0), 1e-30)
    power = jnp.ceil(jnp.log2(largest) * 256.0)
    scale = jnp.exp2(power * (-1.0 / 256.0)) * TOP
    coded = jnp.round(groups * scale[None]).reshape(128, 128)
    return coded.astype(jnp.int32).astype(jnp.int16), power


def store_wave(ref, real, imag):
    coded_real, power_real = encode(real)
    coded_imag, power_imag = encode(imag)
    ref[0:128, :] = coded_real
    ref[128:256, :] = coded_imag
    powers = jnp.concatenate([power_real, power_imag], axis=0)
    ref[256:272, :] = powers.astype(jnp.int32).astype(jnp.int16)


def decode(coded):
    numbers = coded.astype(jnp.int32).astype(jnp.float32)
    scales = jnp.exp2(numbers[256:272] * (1.0 / 256.0)) * (1.0 / TOP)
    real = (numbers[0:128].reshape(16, 8, 128) * scales[0:8][None]).reshape(128, 128)
    imag = (numbers[128:256].reshape(16, 8, 128) * scales[8:16][None]).reshape(128, 128)
    return real, imag


def split(value):
    high = value.astype(jnp.bfloat16)
    return high, (value - high.astype(jnp.float32)).astype(jnp.bfloat16)


def dot(a, b):
    return jnp.dot(a, b, preferred_element_type=jnp.float32)


def kernel(
    own, fronts, probe, obj, right_high, right_low, left_high, left_low, lists, out,
    fronts_v, probe_v, obj_b, obj_f, lists_v, lists_s, send0, waves, made, back,
    local_sem, list_send, list_recv, in_send, in_recv, hop_send, hop_recv, out_send, out_recv,
):
    d = lax.axis_index("depth")
    u = lax.axis_index("tile")
    n_depth = lax.axis_size("depth")

    barrier = pltpu.get_barrier_semaphore()
    for j in range(1, 8):
        pl.semaphore_signal(barrier, inc=1, device_id=(d, lax.rem(u + j, 8)), device_id_type=MESH)
    pl.semaphore_signal(barrier, inc=1, device_id=(lax.rem(d + 1, n_depth), u), device_id_type=MESH)
    pl.semaphore_signal(barrier, inc=1, device_id=(lax.rem(d + n_depth - 1, n_depth), u), device_id_type=MESH)

    get_fronts = pltpu.make_async_copy(fronts, fronts_v, local_sem.at[0])
    get_probe = pltpu.make_async_copy(probe, probe_v, local_sem.at[1])
    get_obj = pltpu.make_async_copy(obj, obj_b, local_sem.at[2])
    get_fronts.start()
    get_probe.start()
    get_obj.start()

    get_fronts.wait()

    @pl.loop(0, 8)
    def _(j):
        wave = fronts_v[own[j]]

        @pl.when(j == 0)
        def _():
            store_wave(waves.at[0, 0], wave[0], wave[1])

        @pl.when(j > 0)
        def _():
            store_wave(send0.at[j], wave[0], wave[1])

    get_probe.wait()

    @pl.when(d == 0)
    def _():
        @pl.loop(0, 8)
        def _(j):
            for s in range(1, STEPS):
                store_wave(waves.at[s, j], probe_v[0], probe_v[1])

    pl.semaphore_wait(barrier, 9)

    def list_copy(j):
        return pltpu.make_async_remote_copy(
            lists.at[j], lists_v.at[j], list_send.at[j], list_recv.at[j],
            device_id=(d, lax.rem(u + 8 - offset_of(j), 8)), device_id_type=MESH)

    def in_copy(j):
        return pltpu.make_async_remote_copy(
            send0.at[j], waves.at[0, j], in_send.at[j], in_recv.at[j],
            device_id=(d, lax.rem(u + 8 - offset_of(j), 8)), device_id_type=MESH)

    def hop_copy(s, pair):
        return pltpu.make_async_remote_copy(
            made.at[s, pl.ds(2 * pair, 2)], waves.at[s + 1, pl.ds(2 * pair, 2)],
            hop_send.at[s, pair], hop_recv.at[s, pair],
            device_id=(lax.rem(d + 1, n_depth), u), device_id_type=MESH)

    def out_copy(j):
        return pltpu.make_async_remote_copy(
            made.at[3, j], back.at[j], out_send.at[j], out_recv.at[j],
            device_id=(d, lax.rem(u + offset_of(j), 8)), device_id_type=MESH)

    @pl.loop(1, 8)
    def _(j):
        list_copy(j).start()

    @pl.loop(1, 8)
    def _(j):
        in_copy(j).start()

    lists_v[0] = lists[0]

    get_obj.wait()
    for layer in range(2):
        for part in range(2):
            for third in range(3):
                obj_f[layer, part, third] = obj_b[layer, part, :, third * 128:(third + 1) * 128].astype(jnp.float32)

    @pl.loop(1, 8)
    def _(j):
        list_copy(j).wait()

    get_lists = pltpu.make_async_copy(lists_v, lists_s, local_sem.at[3])
    get_lists.start()
    get_lists.wait()

    lane = lax.broadcasted_iota(jnp.int32, (128, 128), 1)

    def cut(layer, part, row, column):
        third = lax.shift_right_logical(column, 7)
        left = lax.bitwise_and(column, 127)
        first = obj_f[layer, part, third, pl.ds(row, 128), :]
        second = obj_f[layer, part, jnp.minimum(third + 1, 2), pl.ds(row, 128), :]
        mixed = jnp.where(lane >= left, first, second)
        return pltpu.roll(mixed, lax.bitwise_and(128 - left, 127), 1)

    def one_task(s, pair):
        @pl.when(s == 0)
        def _():
            @pl.when(pair > 0)
            def _():
                in_copy(2 * pair).wait_recv()

            in_copy(2 * pair + 1).wait_recv()

        @pl.when((s > 0) & (d > 0))
        def _():
            hop_copy(s - 1, pair).wait_recv()

        real = [None, None]
        imag = [None, None]
        for side in range(2):
            real[side], imag[side] = decode(waves[s, 2 * pair + side])
        for layer in range(2):
            for side in range(2):
                row = lists_s[2 * pair + side, 0, s]
                column = lists_s[2 * pair + side, 0, 4 + s]
                trans_real = cut(layer, 0, row, column)
                trans_imag = cut(layer, 1, row, column)
                real[side], imag[side] = (
                    real[side] * trans_real - imag[side] * trans_imag,
                    real[side] * trans_imag + imag[side] * trans_real,
                )
            high, low = split(jnp.concatenate([
                jnp.concatenate([real[0], imag[0]], axis=1),
                jnp.concatenate([real[1], imag[1]], axis=1),
            ], axis=0))
            got = dot(high, right_high[...]) + dot(high, right_low[...]) + dot(low, right_high[...])
            high, low = split(jnp.concatenate([
                jnp.concatenate([got[0:128, 0:128], got[128:256, 0:128]], axis=1),
                jnp.concatenate([got[0:128, 128:256], got[128:256, 128:256]], axis=1),
            ], axis=0))
            got = dot(left_high[...], high) + dot(left_low[...], high) + dot(left_high[...], low)
            for side in range(2):
                real[side] = got[0:128, side * 128:(side + 1) * 128]
                imag[side] = got[128:256, side * 128:(side + 1) * 128]
        for side in range(2):
            store_wave(made.at[s, 2 * pair + side], real[side], imag[side])

        @pl.when((s < 3) & (d < n_depth - 1))
        def _():
            hop_copy(s, pair).start()

        @pl.when(s == 3)
        def _():
            @pl.when(pair > 0)
            def _():
                out_copy(2 * pair).start()

            @pl.when(pair == 0)
            def _():
                back[0] = made[3, 0]

            out_copy(2 * pair + 1).start()

    @pl.loop(0, 7)
    def _(g):
        @pl.loop(0, 4)
        def _(i):
            s = 3 - i
            pair = g - s

            @pl.when((pair >= 0) & (pair < 4))
            def _():
                one_task(s, pair)

    @pl.loop(1, 8)
    def _(j):
        in_copy(j).wait_send()
        out_copy(j).wait()

    @pl.when(d < n_depth - 1)
    def _():
        @pl.loop(0, 3)
        def _(s):
            @pl.loop(0, 4)
            def _(pair):
                hop_copy(s, pair).wait_send()

    @pl.loop(0, 8)
    def _(p):
        real, imag = decode(back[own[8 + p]])
        live = own[16 + p] > 0
        out[p, 0] = jnp.where(live, real, 0.0)
        out[p, 1] = jnp.where(live, imag, 0.0)


def per_device(fronts, probe_wave, object_slices, patch_list, counts):
    d = lax.axis_index("depth")
    t = lax.axis_index("tile")
    first = lax.axis_size("depth") - 1 - d
    listed = lax.dynamic_slice(patch_list[:, 0], (first, 0, 0), (STEPS, 3, 8))
    count = lax.dynamic_slice(counts[:, 0], (first,), (STEPS,))
    probes = jnp.arange(8, dtype=jnp.int32)
    offset = lax.rem(t - listed[:, 0] + 8, 8)
    slot = jnp.where(offset == 0, 0, jnp.where(offset <= 4, 2 * offset - 1, 16 - 2 * offset))
    live = probes[None] < count[:, None]
    chosen = (live[:, None] & (slot[:, None] == probes[None, :, None])).astype(jnp.int32)
    rows = jnp.sum(chosen * listed[:, 1][:, None], axis=-1)
    columns = jnp.sum(chosen * listed[:, 2][:, None], axis=-1)
    source = jnp.sum(chosen[0] * probes[None], axis=-1)
    own = jnp.concatenate([source, slot[3], live[3].astype(jnp.int32)])
    lists = jnp.concatenate([rows, columns], axis=0).T
    lists = jnp.pad(lists[:, None, :], ((0, 0), (0, 7), (0, 120)))
    tables = propagator(128)
    any_space = pl.BlockSpec(memory_space=pl.ANY)
    vmem = pl.BlockSpec(memory_space=pltpu.VMEM)
    result = pl.pallas_call(
        kernel,
        out_shape=jax.ShapeDtypeStruct((8, 2, 128, 128), jnp.float32),
        in_specs=[pl.BlockSpec(memory_space=pltpu.SMEM), any_space, any_space, any_space, vmem, vmem, vmem, vmem, vmem],
        out_specs=vmem,
        scratch_shapes=[
            pltpu.VMEM((8, 2, 128, 128), jnp.float32),
            pltpu.VMEM((2, 128, 128), jnp.float32),
            pltpu.VMEM((2, 2, 384, 384), jnp.bfloat16),
            pltpu.VMEM((2, 2, 3, 384, 128), jnp.float32),
            pltpu.VMEM((8, 8, 128), jnp.int32),
            pltpu.SMEM((8, 8, 128), jnp.int32),
            pltpu.VMEM((8, ROWS, 128), jnp.int16),
            pltpu.VMEM((STEPS, 8, ROWS, 128), jnp.int16),
            pltpu.VMEM((STEPS, 8, ROWS, 128), jnp.int16),
            pltpu.VMEM((8, ROWS, 128), jnp.int16),
            pltpu.SemaphoreType.DMA((4,)),
            pltpu.SemaphoreType.DMA((8,)),
            pltpu.SemaphoreType.DMA((8,)),
            pltpu.SemaphoreType.DMA((8,)),
            pltpu.SemaphoreType.DMA((8,)),
            pltpu.SemaphoreType.DMA((3, 4)),
            pltpu.SemaphoreType.DMA((3, 4)),
            pltpu.SemaphoreType.DMA((8,)),
            pltpu.SemaphoreType.DMA((8,)),
        ],
        compiler_params=pltpu.CompilerParams(
            collective_id=0, has_side_effects=True, vmem_limit_bytes=40 * 1024 * 1024
        ),
    )(own, fronts[0, 0], probe_wave, object_slices, *[jnp.asarray(x) for x in tables], lists)
    return result[None, None]


def solution(mesh):
    in_specs = (
        P("depth", "tile", None, None, None, None),
        P(),
        P("depth", None, "tile", None),
        P(None, "tile", None, None),
        P(None, "tile"),
    )
    out_specs = P("depth", "tile", None, None, None, None)
    return jax.shard_map(
        per_device, mesh=mesh, in_specs=in_specs, out_specs=out_specs, check_vma=False
    )
```

```python
import functools
import math

import jax
import jax.numpy as jnp
import ml_dtypes
import numpy as np
from jax import lax
from jax.experimental import pallas as pl
from jax.experimental.pallas import tpu as pltpu
from jax.sharding import PartitionSpec as P

STEPS = 4
FRESNEL_RATE = 0.3
MESH = pl.DeviceIdType.MESH

ROWS = 272
TOP = 32766.0


def split_table(table):
    high = table.astype(ml_dtypes.bfloat16)
    low = (table - high.astype(np.float64)).astype(ml_dtypes.bfloat16)
    return high, low


def propagator(width):
    index = np.arange(width)
    angle = 2.0 * math.pi / width * ((index[:, None] * index[None, :]) % width)
    forward = np.cos(angle) - 1j * np.sin(angle)
    inverse = (np.cos(angle) + 1j * np.sin(angle)) / width
    freq = np.where(index < width // 2, index, index - width).astype(np.float64)
    phase = -2.0 * math.pi * FRESNEL_RATE / width * freq**2
    matrix = inverse @ ((np.cos(phase) + 1j * np.sin(phase))[:, None] * forward)
    real, imag = matrix.real, matrix.imag
    right = np.block([[real, imag], [-imag, real]])
    left = np.block([[real, -imag], [imag, real]])
    return split_table(right) + split_table(left)


def offset_of(slot):
    pair = slot // 2
    return lax.rem(16 + (lax.rem(pair, 2) * 2 - 1) * ((pair + 1) // 2) + 4 * lax.rem(slot, 2), 8)


def slot_of(offset):
    side = jnp.where((offset >= 3) & (offset <= 6), 1, 0)
    base = (offset + 4 * side) % 8
    return 2 * jnp.where(base == 7, 2, jnp.where(base == 2, 3, base)) + side


def encode(plane):
    groups = plane.reshape(16, 8, 128)
    largest = jnp.maximum(jnp.max(jnp.abs(groups), axis=0), 1e-30)
    power = jnp.ceil(jnp.log2(largest) * 256.0)
    scale = jnp.exp2(power * (-1.0 / 256.0)) * TOP
    coded = jnp.round(groups * scale[None]).reshape(128, 128)
    return coded.astype(jnp.int32).astype(jnp.int16), power


def store_wave(ref, real, imag):
    coded_real, power_real = encode(real)
    coded_imag, power_imag = encode(imag)
    ref[0:128, :] = coded_real
    ref[128:256, :] = coded_imag
    powers = jnp.concatenate([power_real, power_imag], axis=0)
    ref[256:272, :] = powers.astype(jnp.int32).astype(jnp.int16)


def decode(coded):
    numbers = coded.astype(jnp.int32).astype(jnp.float32)
    scales = jnp.exp2(numbers[256:272] * (1.0 / 256.0)) * (1.0 / TOP)
    real = (numbers[0:128].reshape(16, 8, 128) * scales[0:8][None]).reshape(128, 128)
    imag = (numbers[128:256].reshape(16, 8, 128) * scales[8:16][None]).reshape(128, 128)
    return real, imag


def split(value):
    high = value.astype(jnp.bfloat16)
    return high, (value - high.astype(jnp.float32)).astype(jnp.bfloat16)


def dot(a, b):
    return jnp.dot(a, b, preferred_element_type=jnp.float32)


def kernel(
    listed, counts, fronts, probe, obj, tables, out,
    listed_s, counts_s, listed_v, counts_v, tables_v, fronts_v, probe_v, obj_b, obj_f,
    lists, lists_v, lists_s, send0, waves, made, back,
    local_sem, list_send, list_recv, in_send, in_recv, hop_send, hop_recv, out_send, out_recv,
):
    d = lax.axis_index("depth")
    u = lax.axis_index("tile")
    n_depth = lax.axis_size("depth")
    batches = listed.shape[-1]

    barrier = pltpu.get_barrier_semaphore()
    for j in range(1, 8):
        pl.semaphore_signal(barrier, inc=1, device_id=(d, lax.rem(u + j, 8)), device_id_type=MESH)
    pl.semaphore_signal(barrier, inc=1, device_id=(lax.rem(d + 1, n_depth), u), device_id_type=MESH)
    pl.semaphore_signal(barrier, inc=1, device_id=(lax.rem(d + n_depth - 1, n_depth), u), device_id_type=MESH)

    pairs = ((listed, listed_v), (counts, counts_v), (listed, listed_s), (counts, counts_s), (fronts, fronts_v),
             (probe, probe_v), (obj, obj_b), (tables, tables_v))
    gets = [pltpu.make_async_copy(a, b, local_sem.at[i]) for i, (a, b) in enumerate(pairs)]
    for get in gets:
        get.start()

    first = n_depth - 1 - d
    gets[0].wait()
    gets[1].wait()
    probes = lax.broadcasted_iota(jnp.int32, (8, batches), 0)
    live = probes < counts_v[...]
    slots = jnp.where(live, slot_of(lax.rem(u - listed_v[0] + 8, 8)), -1)
    for j in range(8):
        chosen = slots == j
        for field in range(2):
            lists[j, field:field + 1, :] = jnp.sum(
                jnp.where(chosen, listed_v[1 + field], 0), axis=0, keepdims=True)

    for get in gets[2:5]:
        get.wait()

    @pl.loop(0, 8)
    def _(j):
        target = lax.rem(u + 8 - offset_of(j), 8)
        count = counts_s[0, first]
        source = jnp.int32(0)
        for p in range(8):
            source = jnp.where((listed_s[0, p, first] == target) & (p < count), p, source)
        wave = fronts_v[source]

        @pl.when(j == 0)
        def _():
            store_wave(waves.at[0, 0], wave[0], wave[1])

        @pl.when(j > 0)
        def _():
            store_wave(send0.at[j], wave[0], wave[1])

    gets[5].wait()

    @pl.when(d == 0)
    def _():
        @pl.loop(0, 8)
        def _(j):
            for s in range(1, STEPS):
                store_wave(waves.at[s, j], probe_v[0], probe_v[1])

    pl.semaphore_wait(barrier, 9)

    def list_copy(j):
        return pltpu.make_async_remote_copy(
            lists.at[j], lists_v.at[j], list_send.at[j], list_recv.at[j],
            device_id=(d, lax.rem(u + 8 - offset_of(j), 8)), device_id_type=MESH)

    def in_copy(j):
        return pltpu.make_async_remote_copy(
            send0.at[j], waves.at[0, j], in_send.at[j], in_recv.at[j],
            device_id=(d, lax.rem(u + 8 - offset_of(j), 8)), device_id_type=MESH)

    def hop_copy(s, pair):
        return pltpu.make_async_remote_copy(
            made.at[s, pl.ds(2 * pair, 2)], waves.at[s + 1, pl.ds(2 * pair, 2)],
            hop_send.at[s, pair], hop_recv.at[s, pair],
            device_id=(lax.rem(d + 1, n_depth), u), device_id_type=MESH)

    def out_copy(j):
        return pltpu.make_async_remote_copy(
            made.at[3, j], back.at[j], out_send.at[j], out_recv.at[j],
            device_id=(d, lax.rem(u + offset_of(j), 8)), device_id_type=MESH)

    @pl.loop(1, 8)
    def _(j):
        list_copy(j).start()

    @pl.loop(1, 8)
    def _(j):
        in_copy(j).start()

    lists_v[0] = lists[0]

    gets[6].wait()
    for layer in range(2):
        for part in range(2):
            for third in range(3):
                obj_f[layer, part, third] = obj_b[layer, part, :, third * 128:(third + 1) * 128].astype(jnp.float32)

    @pl.loop(1, 8)
    def _(j):
        list_copy(j).wait()

    get_lists = pltpu.make_async_copy(lists_v, lists_s, local_sem.at[8])
    get_lists.start()
    get_lists.wait()
    gets[7].wait()

    lane = lax.broadcasted_iota(jnp.int32, (128, 128), 1)

    def cut(layer, part, row, column):
        third = lax.shift_right_logical(column, 7)
        left = lax.bitwise_and(column, 127)
        first = obj_f[layer, part, third, pl.ds(row, 128), :]
        second = obj_f[layer, part, jnp.minimum(third + 1, 2), pl.ds(row, 128), :]
        mixed = jnp.where(lane >= left, first, second)
        return pltpu.roll(mixed, lax.bitwise_and(128 - left, 127), 1)

    def one_task(s, pair):
        @pl.when(s == 0)
        def _():
            @pl.when(pair > 0)
            def _():
                in_copy(2 * pair).wait_recv()

            in_copy(2 * pair + 1).wait_recv()

        @pl.when((s > 0) & (d > 0))
        def _():
            hop_copy(s - 1, pair).wait_recv()

        real = [None, None]
        imag = [None, None]
        for side in range(2):
            real[side], imag[side] = decode(waves[s, 2 * pair + side])
        for layer in range(2):
            for side in range(2):
                row = lists_s[2 * pair + side, 0, first + s]
                column = lists_s[2 * pair + side, 1, first + s]
                trans_real = cut(layer, 0, row, column)
                trans_imag = cut(layer, 1, row, column)
                real[side], imag[side] = (
                    real[side] * trans_real - imag[side] * trans_imag,
                    real[side] * trans_imag + imag[side] * trans_real,
                )
            high, low = split(jnp.concatenate([
                jnp.concatenate([real[0], imag[0]], axis=1),
                jnp.concatenate([real[1], imag[1]], axis=1),
            ], axis=0))
            got = dot(high, tables_v[0]) + dot(high, tables_v[1]) + dot(low, tables_v[0])
            high, low = split(jnp.concatenate([
                jnp.concatenate([got[0:128, 0:128], got[128:256, 0:128]], axis=1),
                jnp.concatenate([got[0:128, 128:256], got[128:256, 128:256]], axis=1),
            ], axis=0))
            got = dot(tables_v[2], high) + dot(tables_v[3], high) + dot(tables_v[2], low)
            for side in range(2):
                real[side] = got[0:128, side * 128:(side + 1) * 128]
                imag[side] = got[128:256, side * 128:(side + 1) * 128]
        for side in range(2):
            store_wave(made.at[s, 2 * pair + side], real[side], imag[side])

        @pl.when((s < 3) & (d < n_depth - 1))
        def _():
            hop_copy(s, pair).start()

        @pl.when(s == 3)
        def _():
            @pl.when(pair > 0)
            def _():
                out_copy(2 * pair).start()

            @pl.when(pair == 0)
            def _():
                back[0] = made[3, 0]

            out_copy(2 * pair + 1).start()

    @pl.loop(0, 7)
    def _(g):
        @pl.loop(0, 4)
        def _(i):
            s = i
            pair = g - s

            @pl.when((pair >= 0) & (pair < 4))
            def _():
                one_task(s, pair)

    @pl.loop(1, 8)
    def _(j):
        in_copy(j).wait_send()
        out_copy(j).wait()

    @pl.when(d < n_depth - 1)
    def _():
        @pl.loop(0, 3)
        def _(s):
            @pl.loop(0, 4)
            def _(pair):
                hop_copy(s, pair).wait_send()

    @pl.loop(0, 8)
    def _(p):
        last = first + STEPS - 1
        real, imag = decode(back[slot_of(lax.rem(u - listed_s[0, p, last] + 8, 8))])
        live = p < counts_s[0, last]
        out[p, 0] = jnp.where(live, real, 0.0)
        out[p, 1] = jnp.where(live, imag, 0.0)


def per_device(fronts, probe_wave, object_slices, patch_list, counts):
    tables = jnp.asarray(np.stack(propagator(128)))
    batches = counts.shape[0]
    any_space = pl.BlockSpec(memory_space=pl.ANY)
    vmem = pl.BlockSpec(memory_space=pltpu.VMEM)
    result = pl.pallas_call(
        kernel,
        out_shape=jax.ShapeDtypeStruct((8, 2, 128, 128), jnp.float32),
        in_specs=[any_space] * 6,
        out_specs=vmem,
        scratch_shapes=[
            pltpu.SMEM((3, 8, batches), jnp.int32),
            pltpu.SMEM((1, batches), jnp.int32),
            pltpu.VMEM((3, 8, batches), jnp.int32),
            pltpu.VMEM((1, batches), jnp.int32),
            pltpu.VMEM((4, 256, 256), jnp.bfloat16),
            pltpu.VMEM((8, 2, 128, 128), jnp.float32),
            pltpu.VMEM((2, 128, 128), jnp.float32),
            pltpu.VMEM((2, 2, 384, 384), jnp.bfloat16),
            pltpu.VMEM((2, 2, 3, 384, 128), jnp.float32),
            pltpu.VMEM((8, 8, batches), jnp.int32),
            pltpu.VMEM((8, 8, batches), jnp.int32),
            pltpu.SMEM((8, 8, batches), jnp.int32),
            pltpu.VMEM((8, ROWS, 128), jnp.int16),
            pltpu.VMEM((STEPS, 8, ROWS, 128), jnp.int16),
            pltpu.VMEM((STEPS, 8, ROWS, 128), jnp.int16),
            pltpu.VMEM((8, ROWS, 128), jnp.int16),
            pltpu.SemaphoreType.DMA((9,)),
            pltpu.SemaphoreType.DMA((8,)),
            pltpu.SemaphoreType.DMA((8,)),
            pltpu.SemaphoreType.DMA((8,)),
            pltpu.SemaphoreType.DMA((8,)),
            pltpu.SemaphoreType.DMA((3, 4)),
            pltpu.SemaphoreType.DMA((3, 4)),
            pltpu.SemaphoreType.DMA((8,)),
            pltpu.SemaphoreType.DMA((8,)),
        ],
        compiler_params=pltpu.CompilerParams(
            collective_id=0, has_side_effects=True, vmem_limit_bytes=60 * 1024 * 1024
        ),
    )(
        jnp.transpose(patch_list[:, 0], (1, 2, 0)), jnp.transpose(counts), fronts[0, 0], probe_wave, object_slices, tables
    )
    return result[None, None]


def solution(mesh):
    in_specs = (
        P("depth", "tile", None, None, None, None),
        P(),
        P("depth", None, "tile", None),
        P(None, "tile", None, None),
        P(None, "tile"),
    )
    out_specs = P("depth", "tile", None, None, None, None)
    return jax.shard_map(
        per_device, mesh=mesh, in_specs=in_specs, out_specs=out_specs, check_vma=False
    )
```

```python
import functools
import math

import jax
import jax.numpy as jnp
import ml_dtypes
import numpy as np
from jax import lax
from jax.experimental import pallas as pl
from jax.experimental.pallas import tpu as pltpu
from jax.sharding import PartitionSpec as P

STEPS = 4
FRESNEL_RATE = 0.3
MESH = pl.DeviceIdType.MESH

ROWS = 272
TOP = 32766.0


def split_table(table):
    high = table.astype(ml_dtypes.bfloat16)
    low = (table - high.astype(np.float64)).astype(ml_dtypes.bfloat16)
    return high, low


def propagator(width):
    index = np.arange(width)
    angle = 2.0 * math.pi / width * ((index[:, None] * index[None, :]) % width)
    forward = np.cos(angle) - 1j * np.sin(angle)
    inverse = (np.cos(angle) + 1j * np.sin(angle)) / width
    freq = np.where(index < width // 2, index, index - width).astype(np.float64)
    phase = -2.0 * math.pi * FRESNEL_RATE / width * freq**2
    matrix = inverse @ ((np.cos(phase) + 1j * np.sin(phase))[:, None] * forward)
    real, imag = matrix.real, matrix.imag
    right = np.block([[real, imag], [-imag, real]])
    left = np.block([[real, -imag], [imag, real]])
    return split_table(right) + split_table(left)


def offset_of(slot):
    pair = slot // 2
    return lax.rem(16 + (lax.rem(pair, 2) * 2 - 1) * ((pair + 1) // 2) + 4 * lax.rem(slot, 2), 8)


def slot_of(offset):
    side = jnp.where((offset >= 3) & (offset <= 6), 1, 0)
    base = (offset + 4 * side) % 8
    return 2 * jnp.where(base == 7, 2, jnp.where(base == 2, 3, base)) + side


def encode(plane):
    groups = plane.reshape(16, 8, 128)
    largest = jnp.maximum(jnp.max(jnp.abs(groups), axis=0), 1e-30)
    power = jnp.ceil(jnp.log2(largest) * 256.0)
    scale = jnp.exp2(power * (-1.0 / 256.0)) * TOP
    coded = jnp.round(groups * scale[None]).reshape(128, 128)
    return coded.astype(jnp.int32).astype(jnp.int16), power


def store_wave(ref, real, imag):
    coded_real, power_real = encode(real)
    coded_imag, power_imag = encode(imag)
    ref[0:128, :] = coded_real
    ref[128:256, :] = coded_imag
    powers = jnp.concatenate([power_real, power_imag], axis=0)
    ref[256:272, :] = powers.astype(jnp.int32).astype(jnp.int16)


def decode(coded):
    numbers = coded.astype(jnp.int32).astype(jnp.float32)
    scales = jnp.exp2(numbers[256:272] * (1.0 / 256.0)) * (1.0 / TOP)
    real = (numbers[0:128].reshape(16, 8, 128) * scales[0:8][None]).reshape(128, 128)
    imag = (numbers[128:256].reshape(16, 8, 128) * scales[8:16][None]).reshape(128, 128)
    return real, imag


def split(value):
    high = value.astype(jnp.bfloat16)
    return high, (value - high.astype(jnp.float32)).astype(jnp.bfloat16)


def dot(a, b):
    return jnp.dot(a, b, preferred_element_type=jnp.float32)


def kernel(
    listed, counts, fronts, probe, obj, tables, back,
    listed_s, counts_s, listed_v, counts_v, tables_v, fronts_v, probe_v, obj_b, obj_f,
    lists, lists_v, lists_s, send0, waves, made,
    local_sem, list_send, list_recv, in_send, in_recv, hop_send, hop_recv, out_send, out_recv,
):
    d = lax.axis_index("depth")
    u = lax.axis_index("tile")
    n_depth = lax.axis_size("depth")
    batches = listed.shape[-1]

    barrier = pltpu.get_barrier_semaphore()
    for j in range(1, 8):
        pl.semaphore_signal(barrier, inc=1, device_id=(d, lax.rem(u + j, 8)), device_id_type=MESH)
    pl.semaphore_signal(barrier, inc=1, device_id=(lax.rem(d + 1, n_depth), u), device_id_type=MESH)
    pl.semaphore_signal(barrier, inc=1, device_id=(lax.rem(d + n_depth - 1, n_depth), u), device_id_type=MESH)

    pairs = ((listed, listed_v), (counts, counts_v), (listed, listed_s), (counts, counts_s), (fronts, fronts_v),
             (probe, probe_v), (obj, obj_b), (tables, tables_v))
    gets = [pltpu.make_async_copy(a, b, local_sem.at[i]) for i, (a, b) in enumerate(pairs)]
    for get in gets:
        get.start()

    first = n_depth - 1 - d
    gets[0].wait()
    gets[1].wait()
    probes = lax.broadcasted_iota(jnp.int32, (8, batches), 0)
    live = probes < counts_v[...]
    slots = jnp.where(live, slot_of(lax.rem(u - listed_v[0] + 8, 8)), -1)
    for j in range(8):
        chosen = slots == j
        for field in range(2):
            lists[j, field:field + 1, :] = jnp.sum(
                jnp.where(chosen, listed_v[1 + field], 0), axis=0, keepdims=True)

    for get in gets[2:5]:
        get.wait()

    @pl.loop(0, 8)
    def _(j):
        target = lax.rem(u + 8 - offset_of(j), 8)
        count = counts_s[0, first]
        source = jnp.int32(0)
        for p in range(8):
            source = jnp.where((listed_s[0, p, first] == target) & (p < count), p, source)
        wave = fronts_v[source]

        @pl.when(j == 0)
        def _():
            store_wave(waves.at[0, 0], wave[0], wave[1])

        @pl.when(j > 0)
        def _():
            store_wave(send0.at[j], wave[0], wave[1])

    gets[5].wait()

    @pl.when(d == 0)
    def _():
        @pl.loop(0, 8)
        def _(j):
            for s in range(1, STEPS):
                store_wave(waves.at[s, j], probe_v[0], probe_v[1])

    pl.semaphore_wait(barrier, 9)

    def list_copy(j):
        return pltpu.make_async_remote_copy(
            lists.at[j], lists_v.at[j], list_send.at[j], list_recv.at[j],
            device_id=(d, lax.rem(u + 8 - offset_of(j), 8)), device_id_type=MESH)

    def in_copy(j):
        return pltpu.make_async_remote_copy(
            send0.at[j], waves.at[0, j], in_send.at[j], in_recv.at[j],
            device_id=(d, lax.rem(u + 8 - offset_of(j), 8)), device_id_type=MESH)

    def hop_copy(s, pair):
        return pltpu.make_async_remote_copy(
            made.at[s, pl.ds(2 * pair, 2)], waves.at[s + 1, pl.ds(2 * pair, 2)],
            hop_send.at[s, pair], hop_recv.at[s, pair],
            device_id=(lax.rem(d + 1, n_depth), u), device_id_type=MESH)

    def out_copy(j):
        return pltpu.make_async_remote_copy(
            made.at[3, j], back.at[j], out_send.at[j], out_recv.at[j],
            device_id=(d, lax.rem(u + offset_of(j), 8)), device_id_type=MESH)

    @pl.loop(1, 8)
    def _(j):
        list_copy(j).start()

    @pl.loop(1, 8)
    def _(j):
        in_copy(j).start()

    lists_v[0] = lists[0]

    gets[6].wait()
    for layer in range(2):
        for part in range(2):
            for third in range(3):
                obj_f[layer, part, third] = obj_b[layer, part, :, third * 128:(third + 1) * 128].astype(jnp.float32)

    @pl.loop(1, 8)
    def _(j):
        list_copy(j).wait()

    get_lists = pltpu.make_async_copy(lists_v, lists_s, local_sem.at[8])
    get_lists.start()
    get_lists.wait()
    gets[7].wait()

    keep = pltpu.make_async_copy(made.at[3, 0], back.at[0], local_sem.at[9])
    lane = lax.broadcasted_iota(jnp.int32, (128, 128), 1)

    def cut(layer, part, row, column):
        third = lax.shift_right_logical(column, 7)
        left = lax.bitwise_and(column, 127)
        first = obj_f[layer, part, third, pl.ds(row, 128), :]
        second = obj_f[layer, part, jnp.minimum(third + 1, 2), pl.ds(row, 128), :]
        mixed = jnp.where(lane >= left, first, second)
        return pltpu.roll(mixed, lax.bitwise_and(128 - left, 127), 1)

    def one_task(s, pair):
        @pl.when(s == 0)
        def _():
            @pl.when(pair > 0)
            def _():
                in_copy(2 * pair).wait_recv()

            in_copy(2 * pair + 1).wait_recv()

        @pl.when((s > 0) & (d > 0))
        def _():
            hop_copy(s - 1, pair).wait_recv()

        real = [None, None]
        imag = [None, None]
        for side in range(2):
            real[side], imag[side] = decode(waves[s, 2 * pair + side])
        for layer in range(2):
            for side in range(2):
                row = lists_s[2 * pair + side, 0, first + s]
                column = lists_s[2 * pair + side, 1, first + s]
                trans_real = cut(layer, 0, row, column)
                trans_imag = cut(layer, 1, row, column)
                real[side], imag[side] = (
                    real[side] * trans_real - imag[side] * trans_imag,
                    real[side] * trans_imag + imag[side] * trans_real,
                )
            got = []
            for side in range(2):
                high, low = split(jnp.concatenate([real[side], imag[side]], axis=1))
                got.append(dot(high, tables_v[0]) + dot(high, tables_v[1]) + dot(low, tables_v[0]))
            high, low = split(jnp.concatenate([
                jnp.concatenate([got[0][:, 0:128], got[1][:, 0:128]], axis=1),
                jnp.concatenate([got[0][:, 128:256], got[1][:, 128:256]], axis=1),
            ], axis=0))
            got = dot(tables_v[2], high) + dot(tables_v[3], high) + dot(tables_v[2], low)
            for side in range(2):
                real[side] = got[0:128, side * 128:(side + 1) * 128]
                imag[side] = got[128:256, side * 128:(side + 1) * 128]
        for side in range(2):
            store_wave(made.at[s, 2 * pair + side], real[side], imag[side])

        @pl.when((s < 3) & (d < n_depth - 1))
        def _():
            hop_copy(s, pair).start()

        @pl.when(s == 3)
        def _():
            @pl.when(pair > 0)
            def _():
                out_copy(2 * pair).start()

            @pl.when(pair == 0)
            def _():
                keep.start()

            out_copy(2 * pair + 1).start()

    @pl.loop(0, 7)
    def _(g):
        @pl.loop(0, 4)
        def _(i):
            s = i
            pair = g - s

            @pl.when((pair >= 0) & (pair < 4))
            def _():
                one_task(s, pair)

    @pl.loop(1, 8)
    def _(j):
        in_copy(j).wait_send()
        out_copy(j).wait()

    keep.wait()

    @pl.when(d < n_depth - 1)
    def _():
        @pl.loop(0, 3)
        def _(s):
            @pl.loop(0, 4)
            def _(pair):
                hop_copy(s, pair).wait_send()


def finish(listed_s, counts_s, back, out, out_v, sem):
    u = lax.axis_index("tile")
    last = lax.axis_size("depth") - 1 - lax.axis_index("depth") + STEPS - 1

    def put(p):
        return pltpu.make_async_copy(out_v.at[p], out.at[p], sem.at[p])

    @pl.loop(0, 8)
    def _(p):
        real, imag = decode(back[slot_of(lax.rem(u - listed_s[0, p, last] + 8, 8))])
        live = p < counts_s[0, last]
        out_v[p, 0] = jnp.where(live, real, 0.0)
        out_v[p, 1] = jnp.where(live, imag, 0.0)
        put(p).start()

    @pl.loop(0, 8)
    def _(p):
        put(p).wait()


def per_device(fronts, probe_wave, object_slices, patch_list, counts):
    tables = jnp.asarray(np.stack(propagator(128)))
    batches = counts.shape[0]
    any_space = pl.BlockSpec(memory_space=pl.ANY)
    vmem = pl.BlockSpec(memory_space=pltpu.VMEM)
    listed = jnp.transpose(patch_list[:, 0], (1, 2, 0))
    counted = jnp.transpose(counts)
    back = pl.pallas_call(
        kernel,
        out_shape=jax.ShapeDtypeStruct((8, ROWS, 128), jnp.int16),
        in_specs=[any_space] * 6,
        out_specs=any_space,
        scratch_shapes=[
            pltpu.SMEM((3, 8, batches), jnp.int32),
            pltpu.SMEM((1, batches), jnp.int32),
            pltpu.VMEM((3, 8, batches), jnp.int32),
            pltpu.VMEM((1, batches), jnp.int32),
            pltpu.VMEM((4, 256, 256), jnp.bfloat16),
            pltpu.VMEM((8, 2, 128, 128), jnp.float32),
            pltpu.VMEM((2, 128, 128), jnp.float32),
            pltpu.VMEM((2, 2, 384, 384), jnp.bfloat16),
            pltpu.VMEM((2, 2, 3, 384, 128), jnp.float32),
            pltpu.VMEM((8, 8, batches), jnp.int32),
            pltpu.VMEM((8, 8, batches), jnp.int32),
            pltpu.SMEM((8, 8, batches), jnp.int32),
            pltpu.VMEM((8, ROWS, 128), jnp.int16),
            pltpu.VMEM((STEPS, 8, ROWS, 128), jnp.int16),
            pltpu.VMEM((STEPS, 8, ROWS, 128), jnp.int16),
            pltpu.SemaphoreType.DMA((10,)),
            pltpu.SemaphoreType.DMA((8,)),
            pltpu.SemaphoreType.DMA((8,)),
            pltpu.SemaphoreType.DMA((8,)),
            pltpu.SemaphoreType.DMA((8,)),
            pltpu.SemaphoreType.DMA((3, 4)),
            pltpu.SemaphoreType.DMA((3, 4)),
            pltpu.SemaphoreType.DMA((8,)),
            pltpu.SemaphoreType.DMA((8,)),
        ],
        compiler_params=pltpu.CompilerParams(
            collective_id=0, has_side_effects=True, vmem_limit_bytes=60 * 1024 * 1024
        ),
    )(listed, counted, fronts[0, 0], probe_wave, object_slices, tables)
    smem = pl.BlockSpec(memory_space=pltpu.SMEM)
    result = pl.pallas_call(
        finish,
        out_shape=jax.ShapeDtypeStruct((8, 2, 128, 128), jnp.float32),
        in_specs=[smem, smem, vmem],
        out_specs=any_space,
        scratch_shapes=[pltpu.VMEM((8, 2, 128, 128), jnp.float32), pltpu.SemaphoreType.DMA((8,))],
        compiler_params=pltpu.CompilerParams(vmem_limit_bytes=60 * 1024 * 1024),
    )(listed, counted, back)
    return result[None, None]


def solution(mesh):
    in_specs = (
        P("depth", "tile", None, None, None, None),
        P(),
        P("depth", None, "tile", None),
        P(None, "tile", None, None),
        P(None, "tile"),
    )
    out_specs = P("depth", "tile", None, None, None, None)
    return jax.shard_map(
        per_device, mesh=mesh, in_specs=in_specs, out_specs=out_specs, check_vma=False
    )
```

```python
import functools
import math

import jax
import jax.numpy as jnp
import ml_dtypes
import numpy as np
from jax import lax
from jax.experimental import pallas as pl
from jax.experimental.pallas import tpu as pltpu
from jax.sharding import PartitionSpec as P

STEPS = 4
FRESNEL_RATE = 0.3
MESH = pl.DeviceIdType.MESH

ROWS = 272
TOP = 32766.0


def split_table(table):
    high = table.astype(ml_dtypes.bfloat16)
    low = (table - high.astype(np.float64)).astype(ml_dtypes.bfloat16)
    return high, low


def propagator(width):
    index = np.arange(width)
    angle = 2.0 * math.pi / width * ((index[:, None] * index[None, :]) % width)
    forward = np.cos(angle) - 1j * np.sin(angle)
    inverse = (np.cos(angle) + 1j * np.sin(angle)) / width
    freq = np.where(index < width // 2, index, index - width).astype(np.float64)
    phase = -2.0 * math.pi * FRESNEL_RATE / width * freq**2
    matrix = inverse @ ((np.cos(phase) + 1j * np.sin(phase))[:, None] * forward)
    real, imag = matrix.real, matrix.imag
    right = np.block([[real, imag], [-imag, real]])
    left = np.block([[real, -imag], [imag, real]])
    return split_table(right) + split_table(left)


def offset_of(slot):
    pair = slot // 2
    return lax.rem(16 + (lax.rem(pair, 2) * 2 - 1) * ((pair + 1) // 2) + 4 * lax.rem(slot, 2), 8)


def slot_of(offset):
    side = jnp.where((offset >= 3) & (offset <= 6), 1, 0)
    base = (offset + 4 * side) % 8
    return 2 * jnp.where(base == 7, 2, jnp.where(base == 2, 3, base)) + side


def encode(plane):
    groups = plane.reshape(16, 8, 128)
    largest = jnp.maximum(jnp.max(jnp.abs(groups), axis=0), 1e-30)
    power = jnp.ceil(jnp.log2(largest) * 256.0)
    scale = jnp.exp2(power * (-1.0 / 256.0)) * TOP
    coded = jnp.round(groups * scale[None]).reshape(128, 128)
    return coded.astype(jnp.int32).astype(jnp.int16), power


def store_wave(ref, real, imag):
    coded_real, power_real = encode(real)
    coded_imag, power_imag = encode(imag)
    ref[0:128, :] = coded_real
    ref[128:256, :] = coded_imag
    powers = jnp.concatenate([power_real, power_imag], axis=0)
    ref[256:272, :] = powers.astype(jnp.int32).astype(jnp.int16)


def decode(coded):
    numbers = coded.astype(jnp.int32).astype(jnp.float32)
    scales = jnp.exp2(numbers[256:272] * (1.0 / 256.0)) * (1.0 / TOP)
    real = (numbers[0:128].reshape(16, 8, 128) * scales[0:8][None]).reshape(128, 128)
    imag = (numbers[128:256].reshape(16, 8, 128) * scales[8:16][None]).reshape(128, 128)
    return real, imag


def split(value):
    high = value.astype(jnp.bfloat16)
    return high, (value - high.astype(jnp.float32)).astype(jnp.bfloat16)


def dot(a, b):
    return jnp.dot(a, b, preferred_element_type=jnp.float32)


def kernel(
    listed, counts, fronts, probe, obj, tables, back,
    listed_s, counts_s, listed_v, counts_v, tables_v, fronts_v, probe_v, obj_b, obj_f,
    lists, lists_v, lists_s, send0, waves, made,
    local_sem, list_send, list_recv, in_send, in_recv, hop_send, hop_recv, out_send, out_recv,
):
    d = lax.axis_index("depth")
    u = lax.axis_index("tile")
    n_depth = lax.axis_size("depth")
    batches = listed.shape[-1]

    barrier = pltpu.get_barrier_semaphore()
    for j in range(1, 8):
        pl.semaphore_signal(barrier, inc=1, device_id=(d, lax.rem(u + j, 8)), device_id_type=MESH)
    pl.semaphore_signal(barrier, inc=1, device_id=(lax.rem(d + 1, n_depth), u), device_id_type=MESH)
    pl.semaphore_signal(barrier, inc=1, device_id=(lax.rem(d + n_depth - 1, n_depth), u), device_id_type=MESH)

    pairs = ((listed, listed_v), (counts, counts_v), (listed, listed_s), (counts, counts_s), (fronts, fronts_v),
             (probe, probe_v), (obj, obj_b), (tables, tables_v))
    gets = [pltpu.make_async_copy(a, b, local_sem.at[i]) for i, (a, b) in enumerate(pairs)]
    for get in gets:
        get.start()

    first = n_depth - 1 - d
    gets[0].wait()
    gets[1].wait()
    probes = lax.broadcasted_iota(jnp.int32, (8, batches), 0)
    live = probes < counts_v[...]
    slots = jnp.where(live, slot_of(lax.rem(u - listed_v[0] + 8, 8)), -1)
    for j in range(8):
        chosen = slots == j
        for field in range(2):
            lists[j, field:field + 1, :] = jnp.sum(
                jnp.where(chosen, listed_v[1 + field], 0), axis=0, keepdims=True)

    for get in gets[2:5]:
        get.wait()

    @pl.loop(0, 8)
    def _(j):
        target = lax.rem(u + 8 - offset_of(j), 8)
        count = counts_s[0, first]
        source = jnp.int32(0)
        for p in range(8):
            source = jnp.where((listed_s[0, p, first] == target) & (p < count), p, source)
        wave = fronts_v[source]

        @pl.when(j == 0)
        def _():
            store_wave(waves.at[0, 0], wave[0], wave[1])

        @pl.when(j > 0)
        def _():
            store_wave(send0.at[j], wave[0], wave[1])

    gets[5].wait()

    @pl.when(d == 0)
    def _():
        @pl.loop(0, 8)
        def _(j):
            for s in range(1, STEPS):
                store_wave(waves.at[s, j], probe_v[0], probe_v[1])

    pl.semaphore_wait(barrier, 9)

    def list_copy(j):
        return pltpu.make_async_remote_copy(
            lists.at[j], lists_v.at[j], list_send.at[j], list_recv.at[j],
            device_id=(d, lax.rem(u + 8 - offset_of(j), 8)), device_id_type=MESH)

    def in_copy(j):
        return pltpu.make_async_remote_copy(
            send0.at[j], waves.at[0, j], in_send.at[j], in_recv.at[j],
            device_id=(d, lax.rem(u + 8 - offset_of(j), 8)), device_id_type=MESH)

    def hop_copy(s, pair):
        return pltpu.make_async_remote_copy(
            made.at[s, pl.ds(2 * pair, 2)], waves.at[s + 1, pl.ds(2 * pair, 2)],
            hop_send.at[s, pair], hop_recv.at[s, pair],
            device_id=(lax.rem(d + 1, n_depth), u), device_id_type=MESH)

    def out_copy(j):
        return pltpu.make_async_remote_copy(
            made.at[3, j], back.at[j], out_send.at[j], out_recv.at[j],
            device_id=(d, lax.rem(u + offset_of(j), 8)), device_id_type=MESH)

    @pl.loop(1, 8)
    def _(j):
        list_copy(j).start()

    @pl.loop(1, 8)
    def _(j):
        in_copy(j).start()

    lists_v[0] = lists[0]

    gets[6].wait()
    for layer in range(2):
        for part in range(2):
            for third in range(3):
                obj_f[layer, part, third] = obj_b[layer, part, :, third * 128:(third + 1) * 128].astype(jnp.float32)

    @pl.loop(1, 8)
    def _(j):
        list_copy(j).wait()

    get_lists = pltpu.make_async_copy(lists_v, lists_s, local_sem.at[8])
    get_lists.start()
    get_lists.wait()
    gets[7].wait()

    keep = pltpu.make_async_copy(made.at[3, 0], back.at[0], local_sem.at[9])
    lane = lax.broadcasted_iota(jnp.int32, (128, 128), 1)

    def cut(layer, part, row, column):
        third = lax.shift_right_logical(column, 7)
        left = lax.bitwise_and(column, 127)
        first = obj_f[layer, part, third, pl.ds(row, 128), :]
        second = obj_f[layer, part, jnp.minimum(third + 1, 2), pl.ds(row, 128), :]
        mixed = jnp.where(lane >= left, first, second)
        return pltpu.roll(mixed, lax.bitwise_and(128 - left, 127), 1)

    def one_task(s, pair):
        @pl.when(s == 0)
        def _():
            @pl.when(pair > 0)
            def _():
                in_copy(2 * pair).wait_recv()

            in_copy(2 * pair + 1).wait_recv()

        @pl.when((s > 0) & (d > 0))
        def _():
            hop_copy(s - 1, pair).wait_recv()

        real = [None, None]
        imag = [None, None]
        for side in range(2):
            real[side], imag[side] = decode(waves[s, 2 * pair + side])
        for layer in range(2):
            for side in range(2):
                row = lists_s[2 * pair + side, 0, first + s]
                column = lists_s[2 * pair + side, 1, first + s]
                trans_real = cut(layer, 0, row, column)
                trans_imag = cut(layer, 1, row, column)
                real[side], imag[side] = (
                    real[side] * trans_real - imag[side] * trans_imag,
                    real[side] * trans_imag + imag[side] * trans_real,
                )
            got = []
            for side in range(2):
                high, low = split(jnp.concatenate([real[side], imag[side]], axis=1))
                got.append(dot(high, tables_v[0]) + dot(high, tables_v[1]) + dot(low, tables_v[0]))
            high, low = split(jnp.concatenate([
                jnp.concatenate([got[0][:, 0:128], got[1][:, 0:128]], axis=1),
                jnp.concatenate([got[0][:, 128:256], got[1][:, 128:256]], axis=1),
            ], axis=0))
            got = [
                dot(tables_v[2, rows], high) + dot(tables_v[3, rows], high) + dot(tables_v[2, rows], low)
                for rows in (pl.ds(0, 128), pl.ds(128, 128))
            ]
            for side in range(2):
                real[side] = got[0][:, side * 128:(side + 1) * 128]
                imag[side] = got[1][:, side * 128:(side + 1) * 128]
        for side in range(2):
            store_wave(made.at[s, 2 * pair + side], real[side], imag[side])

        @pl.when((s < 3) & (d < n_depth - 1))
        def _():
            hop_copy(s, pair).start()

        @pl.when(s == 3)
        def _():
            @pl.when(pair > 0)
            def _():
                out_copy(2 * pair).start()

            @pl.when(pair == 0)
            def _():
                keep.start()

            out_copy(2 * pair + 1).start()

    @pl.loop(0, 7)
    def _(g):
        @pl.loop(0, 4)
        def _(i):
            s = i
            pair = g - s

            @pl.when((pair >= 0) & (pair < 4))
            def _():
                one_task(s, pair)

    @pl.loop(1, 8)
    def _(j):
        in_copy(j).wait_send()
        out_copy(j).wait()

    keep.wait()

    @pl.when(d < n_depth - 1)
    def _():
        @pl.loop(0, 3)
        def _(s):
            @pl.loop(0, 4)
            def _(pair):
                hop_copy(s, pair).wait_send()


def finish(listed_s, counts_s, back, out, out_v, sem):
    u = lax.axis_index("tile")
    last = lax.axis_size("depth") - 1 - lax.axis_index("depth") + STEPS - 1

    def put(p):
        return pltpu.make_async_copy(out_v.at[p], out.at[p], sem.at[p])

    @pl.loop(0, 8)
    def _(p):
        real, imag = decode(back[slot_of(lax.rem(u - listed_s[0, p, last] + 8, 8))])
        live = p < counts_s[0, last]
        out_v[p, 0] = jnp.where(live, real, 0.0)
        out_v[p, 1] = jnp.where(live, imag, 0.0)
        put(p).start()

    @pl.loop(0, 8)
    def _(p):
        put(p).wait()


def per_device(fronts, probe_wave, object_slices, patch_list, counts):
    tables = jnp.asarray(np.stack(propagator(128)))
    batches = counts.shape[0]
    any_space = pl.BlockSpec(memory_space=pl.ANY)
    vmem = pl.BlockSpec(memory_space=pltpu.VMEM)
    listed = jnp.transpose(patch_list[:, 0], (1, 2, 0))
    counted = jnp.transpose(counts)
    back = pl.pallas_call(
        kernel,
        out_shape=jax.ShapeDtypeStruct((8, ROWS, 128), jnp.int16),
        in_specs=[any_space] * 6,
        out_specs=any_space,
        scratch_shapes=[
            pltpu.SMEM((3, 8, batches), jnp.int32),
            pltpu.SMEM((1, batches), jnp.int32),
            pltpu.VMEM((3, 8, batches), jnp.int32),
            pltpu.VMEM((1, batches), jnp.int32),
            pltpu.VMEM((4, 256, 256), jnp.bfloat16),
            pltpu.VMEM((8, 2, 128, 128), jnp.float32),
            pltpu.VMEM((2, 128, 128), jnp.float32),
            pltpu.VMEM((2, 2, 384, 384), jnp.bfloat16),
            pltpu.VMEM((2, 2, 3, 384, 128), jnp.float32),
            pltpu.VMEM((8, 8, batches), jnp.int32),
            pltpu.VMEM((8, 8, batches), jnp.int32),
            pltpu.SMEM((8, 8, batches), jnp.int32),
            pltpu.VMEM((8, ROWS, 128), jnp.int16),
            pltpu.VMEM((STEPS, 8, ROWS, 128), jnp.int16),
            pltpu.VMEM((STEPS, 8, ROWS, 128), jnp.int16),
            pltpu.SemaphoreType.DMA((10,)),
            pltpu.SemaphoreType.DMA((8,)),
            pltpu.SemaphoreType.DMA((8,)),
            pltpu.SemaphoreType.DMA((8,)),
            pltpu.SemaphoreType.DMA((8,)),
            pltpu.SemaphoreType.DMA((3, 4)),
            pltpu.SemaphoreType.DMA((3, 4)),
            pltpu.SemaphoreType.DMA((8,)),
            pltpu.SemaphoreType.DMA((8,)),
        ],
        compiler_params=pltpu.CompilerParams(
            collective_id=0, has_side_effects=True, vmem_limit_bytes=60 * 1024 * 1024
        ),
    )(listed, counted, fronts[0, 0], probe_wave, object_slices, tables)
    smem = pl.BlockSpec(memory_space=pltpu.SMEM)
    result = pl.pallas_call(
        finish,
        out_shape=jax.ShapeDtypeStruct((8, 2, 128, 128), jnp.float32),
        in_specs=[smem, smem, vmem],
        out_specs=any_space,
        scratch_shapes=[pltpu.VMEM((8, 2, 128, 128), jnp.float32), pltpu.SemaphoreType.DMA((8,))],
        compiler_params=pltpu.CompilerParams(vmem_limit_bytes=60 * 1024 * 1024),
    )(listed, counted, back)
    return result[None, None]


def solution(mesh):
    in_specs = (
        P("depth", "tile", None, None, None, None),
        P(),
        P("depth", None, "tile", None),
        P(None, "tile", None, None),
        P(None, "tile"),
    )
    out_specs = P("depth", "tile", None, None, None, None)
    return jax.shard_map(
        per_device, mesh=mesh, in_specs=in_specs, out_specs=out_specs, check_vma=False
    )
```

```python
import functools
import math

import jax
import jax.numpy as jnp
import ml_dtypes
import numpy as np
from jax import lax
from jax.experimental import pallas as pl
from jax.experimental.pallas import tpu as pltpu
from jax.sharding import PartitionSpec as P

STEPS = 4
FRESNEL_RATE = 0.3
MESH = pl.DeviceIdType.MESH

ROWS = 272
TOP = 32766.0


def split_table(table):
    high = table.astype(ml_dtypes.bfloat16)
    low = (table - high.astype(np.float64)).astype(ml_dtypes.bfloat16)
    return high, low


def propagator(width):
    index = np.arange(width)
    angle = 2.0 * math.pi / width * ((index[:, None] * index[None, :]) % width)
    forward = np.cos(angle) - 1j * np.sin(angle)
    inverse = (np.cos(angle) + 1j * np.sin(angle)) / width
    freq = np.where(index < width // 2, index, index - width).astype(np.float64)
    phase = -2.0 * math.pi * FRESNEL_RATE / width * freq**2
    matrix = inverse @ ((np.cos(phase) + 1j * np.sin(phase))[:, None] * forward)
    real, imag = matrix.real, matrix.imag
    right = np.block([[real, imag], [-imag, real]])
    left = np.block([[real, -imag], [imag, real]])
    return split_table(right) + split_table(left)


def offset_of(slot):
    pair = slot // 2
    return lax.rem(16 + (lax.rem(pair, 2) * 2 - 1) * ((pair + 1) // 2) + 4 * lax.rem(slot, 2), 8)


def slot_of(offset):
    side = jnp.where((offset >= 3) & (offset <= 6), 1, 0)
    base = (offset + 4 * side) % 8
    return 2 * jnp.where(base == 7, 2, jnp.where(base == 2, 3, base)) + side


def encode(plane):
    groups = plane.reshape(16, 8, 128)
    largest = jnp.maximum(jnp.max(jnp.abs(groups), axis=0), 1e-30)
    power = jnp.ceil(jnp.log2(largest) * 256.0)
    scale = jnp.exp2(power * (-1.0 / 256.0)) * TOP
    coded = jnp.round(groups * scale[None]).reshape(128, 128)
    return coded.astype(jnp.int32).astype(jnp.int16), power


def store_wave(ref, real, imag):
    coded_real, power_real = encode(real)
    coded_imag, power_imag = encode(imag)
    ref[0:128, :] = coded_real
    ref[128:256, :] = coded_imag
    powers = jnp.concatenate([power_real, power_imag], axis=0)
    ref[256:272, :] = powers.astype(jnp.int32).astype(jnp.int16)


def decode(coded):
    numbers = coded.astype(jnp.int32).astype(jnp.float32)
    scales = jnp.exp2(numbers[256:272] * (1.0 / 256.0)) * (1.0 / TOP)
    real = (numbers[0:128].reshape(16, 8, 128) * scales[0:8][None]).reshape(128, 128)
    imag = (numbers[128:256].reshape(16, 8, 128) * scales[8:16][None]).reshape(128, 128)
    return real, imag


def split(value):
    high = value.astype(jnp.bfloat16)
    return high, (value - high.astype(jnp.float32)).astype(jnp.bfloat16)


def dot(a, b):
    return jnp.dot(a, b, preferred_element_type=jnp.float32)


def kernel(
    listed, counts, fronts, probe, obj, tables, back,
    listed_s, counts_s, listed_v, counts_v, tables_v, fronts_v, probe_v, obj_b, obj_f,
    lists, lists_v, lists_s, send0, waves, made,
    local_sem, list_send, list_recv, in_send, in_recv, hop_send, hop_recv, out_send, out_recv,
):
    d = lax.axis_index("depth")
    u = lax.axis_index("tile")
    n_depth = lax.axis_size("depth")
    batches = listed.shape[-1]

    barrier = pltpu.get_barrier_semaphore()
    for j in range(1, 8):
        pl.semaphore_signal(barrier, inc=1, device_id=(d, lax.rem(u + j, 8)), device_id_type=MESH)
    pl.semaphore_signal(barrier, inc=1, device_id=(lax.rem(d + 1, n_depth), u), device_id_type=MESH)
    pl.semaphore_signal(barrier, inc=1, device_id=(lax.rem(d + n_depth - 1, n_depth), u), device_id_type=MESH)

    pairs = ((listed, listed_v), (counts, counts_v), (listed, listed_s), (counts, counts_s), (fronts, fronts_v),
             (probe, probe_v), (obj, obj_b), (tables, tables_v))
    gets = [pltpu.make_async_copy(a, b, local_sem.at[i]) for i, (a, b) in enumerate(pairs)]
    for get in gets:
        get.start()

    first = n_depth - 1 - d
    gets[0].wait()
    gets[1].wait()
    probes = lax.broadcasted_iota(jnp.int32, (8, batches), 0)
    live = probes < counts_v[...]
    slots = jnp.where(live, slot_of(lax.rem(u - listed_v[0] + 8, 8)), -1)
    for j in range(8):
        chosen = slots == j
        for field in range(2):
            lists[j, field:field + 1, :] = jnp.sum(
                jnp.where(chosen, listed_v[1 + field], 0), axis=0, keepdims=True)

    for get in gets[2:5]:
        get.wait()

    @pl.loop(0, 8)
    def _(j):
        target = lax.rem(u + 8 - offset_of(j), 8)
        count = counts_s[0, first]
        source = jnp.int32(0)
        for p in range(8):
            source = jnp.where((listed_s[0, p, first] == target) & (p < count), p, source)
        wave = fronts_v[source]

        @pl.when(j == 0)
        def _():
            store_wave(waves.at[0, 0], wave[0], wave[1])

        @pl.when(j > 0)
        def _():
            store_wave(send0.at[j], wave[0], wave[1])

    gets[5].wait()

    @pl.when(d == 0)
    def _():
        @pl.loop(0, 8)
        def _(j):
            for s in range(1, STEPS):
                store_wave(waves.at[s, j], probe_v[0], probe_v[1])

    pl.semaphore_wait(barrier, 9)

    def list_copy(j):
        return pltpu.make_async_remote_copy(
            lists.at[j], lists_v.at[j], list_send.at[j], list_recv.at[j],
            device_id=(d, lax.rem(u + 8 - offset_of(j), 8)), device_id_type=MESH)

    def in_copy(j):
        return pltpu.make_async_remote_copy(
            send0.at[j], waves.at[0, j], in_send.at[j], in_recv.at[j],
            device_id=(d, lax.rem(u + 8 - offset_of(j), 8)), device_id_type=MESH)

    def hop_copy(s, pair):
        return pltpu.make_async_remote_copy(
            made.at[s, pl.ds(2 * pair, 2)], waves.at[s + 1, pl.ds(2 * pair, 2)],
            hop_send.at[s, pair], hop_recv.at[s, pair],
            device_id=(lax.rem(d + 1, n_depth), u), device_id_type=MESH)

    def out_copy(j):
        return pltpu.make_async_remote_copy(
            made.at[3, j], back.at[j], out_send.at[j], out_recv.at[j],
            device_id=(d, lax.rem(u + offset_of(j), 8)), device_id_type=MESH)

    @pl.loop(1, 8)
    def _(j):
        list_copy(j).start()

    @pl.loop(1, 8)
    def _(j):
        in_copy(j).start()

    lists_v[0] = lists[0]

    gets[6].wait()
    for layer in range(2):
        for part in range(2):
            for third in range(3):
                obj_f[layer, part, third] = obj_b[layer, part, :, third * 128:(third + 1) * 128].astype(jnp.float32)

    @pl.loop(1, 8)
    def _(j):
        list_copy(j).wait()

    get_lists = pltpu.make_async_copy(lists_v, lists_s, local_sem.at[8])
    get_lists.start()
    get_lists.wait()
    gets[7].wait()

    keep = pltpu.make_async_copy(made.at[3, 0], back.at[0], local_sem.at[9])
    lane = lax.broadcasted_iota(jnp.int32, (128, 128), 1)

    def cut(layer, part, row, column):
        third = lax.shift_right_logical(column, 7)
        left = lax.bitwise_and(column, 127)
        first = obj_f[layer, part, third, pl.ds(row, 128), :]
        second = obj_f[layer, part, jnp.minimum(third + 1, 2), pl.ds(row, 128), :]
        mixed = jnp.where(lane >= left, first, second)
        return pltpu.roll(mixed, lax.bitwise_and(128 - left, 127), 1)

    def one_task(s, pair):
        @pl.when(s == 0)
        def _():
            @pl.when(pair > 0)
            def _():
                in_copy(2 * pair).wait_recv()

            in_copy(2 * pair + 1).wait_recv()

        @pl.when((s > 0) & (d > 0))
        def _():
            hop_copy(s - 1, pair).wait_recv()

        real = [None, None]
        imag = [None, None]
        for side in range(2):
            real[side], imag[side] = decode(waves[s, 2 * pair + side])
        for layer in range(2):
            for side in range(2):
                row = lists_s[2 * pair + side, 0, first + s]
                column = lists_s[2 * pair + side, 1, first + s]
                trans_real = cut(layer, 0, row, column)
                trans_imag = cut(layer, 1, row, column)
                real[side], imag[side] = (
                    real[side] * trans_real - imag[side] * trans_imag,
                    real[side] * trans_imag + imag[side] * trans_real,
                )
            got = []
            for side in range(2):
                high, low = split(jnp.concatenate([real[side], imag[side]], axis=1))
                got.append(jnp.concatenate([
                    dot(high[i:i + 64], tables_v[0]) + dot(high[i:i + 64], tables_v[1]) + dot(low[i:i + 64], tables_v[0])
                    for i in (0, 64)
                ], axis=0))
            high, low = split(jnp.concatenate([
                jnp.concatenate([got[0][:, 0:128], got[1][:, 0:128]], axis=1),
                jnp.concatenate([got[0][:, 128:256], got[1][:, 128:256]], axis=1),
            ], axis=0))
            got = [
                dot(tables_v[2, rows], high) + dot(tables_v[3, rows], high) + dot(tables_v[2, rows], low)
                for rows in (pl.ds(0, 64), pl.ds(64, 64), pl.ds(128, 64), pl.ds(192, 64))
            ]
            got = [jnp.concatenate(got[0:2], axis=0), jnp.concatenate(got[2:4], axis=0)]
            for side in range(2):
                real[side] = got[0][:, side * 128:(side + 1) * 128]
                imag[side] = got[1][:, side * 128:(side + 1) * 128]
        for side in range(2):
            store_wave(made.at[s, 2 * pair + side], real[side], imag[side])

        @pl.when((s < 3) & (d < n_depth - 1))
        def _():
            hop_copy(s, pair).start()

        @pl.when(s == 3)
        def _():
            @pl.when(pair > 0)
            def _():
                out_copy(2 * pair).start()

            @pl.when(pair == 0)
            def _():
                keep.start()

            out_copy(2 * pair + 1).start()

    @pl.loop(0, 7)
    def _(g):
        @pl.loop(0, 4)
        def _(i):
            s = i
            pair = g - s

            @pl.when((pair >= 0) & (pair < 4))
            def _():
                one_task(s, pair)

    @pl.loop(1, 8)
    def _(j):
        in_copy(j).wait_send()
        out_copy(j).wait()

    keep.wait()

    @pl.when(d < n_depth - 1)
    def _():
        @pl.loop(0, 3)
        def _(s):
            @pl.loop(0, 4)
            def _(pair):
                hop_copy(s, pair).wait_send()


def finish(listed_s, counts_s, back, out, out_v, sem):
    u = lax.axis_index("tile")
    last = lax.axis_size("depth") - 1 - lax.axis_index("depth") + STEPS - 1

    def put(p):
        return pltpu.make_async_copy(out_v.at[p], out.at[p], sem.at[p])

    @pl.loop(0, 8)
    def _(p):
        real, imag = decode(back[slot_of(lax.bitwise_and(u - listed_s[0, p, last], 7))])
        live = p < counts_s[0, last]
        out_v[p, 0] = jnp.where(live, real, 0.0)
        out_v[p, 1] = jnp.where(live, imag, 0.0)
        put(p).start()

    @pl.loop(0, 8)
    def _(p):
        put(p).wait()


def per_device(fronts, probe_wave, object_slices, patch_list, counts):
    tables = jnp.asarray(np.stack(propagator(128)))
    batches = counts.shape[0]
    any_space = pl.BlockSpec(memory_space=pl.ANY)
    vmem = pl.BlockSpec(memory_space=pltpu.VMEM)
    listed = jnp.transpose(patch_list[:, 0], (1, 2, 0))
    counted = jnp.transpose(counts)
    back = pl.pallas_call(
        kernel,
        out_shape=jax.ShapeDtypeStruct((8, ROWS, 128), jnp.int16),
        in_specs=[any_space] * 6,
        out_specs=any_space,
        scratch_shapes=[
            pltpu.SMEM((3, 8, batches), jnp.int32),
            pltpu.SMEM((1, batches), jnp.int32),
            pltpu.VMEM((3, 8, batches), jnp.int32),
            pltpu.VMEM((1, batches), jnp.int32),
            pltpu.VMEM((4, 256, 256), jnp.bfloat16),
            pltpu.VMEM((8, 2, 128, 128), jnp.float32),
            pltpu.VMEM((2, 128, 128), jnp.float32),
            pltpu.VMEM((2, 2, 384, 384), jnp.bfloat16),
            pltpu.VMEM((2, 2, 3, 384, 128), jnp.float32),
            pltpu.VMEM((8, 8, batches), jnp.int32),
            pltpu.VMEM((8, 8, batches), jnp.int32),
            pltpu.SMEM((8, 8, batches), jnp.int32),
            pltpu.VMEM((8, ROWS, 128), jnp.int16),
            pltpu.VMEM((STEPS, 8, ROWS, 128), jnp.int16),
            pltpu.VMEM((STEPS, 8, ROWS, 128), jnp.int16),
            pltpu.SemaphoreType.DMA((10,)),
            pltpu.SemaphoreType.DMA((8,)),
            pltpu.SemaphoreType.DMA((8,)),
            pltpu.SemaphoreType.DMA((8,)),
            pltpu.SemaphoreType.DMA((8,)),
            pltpu.SemaphoreType.DMA((3, 4)),
            pltpu.SemaphoreType.DMA((3, 4)),
            pltpu.SemaphoreType.DMA((8,)),
            pltpu.SemaphoreType.DMA((8,)),
        ],
        compiler_params=pltpu.CompilerParams(
            collective_id=0, has_side_effects=True, vmem_limit_bytes=60 * 1024 * 1024
        ),
    )(listed, counted, fronts[0, 0], probe_wave, object_slices, tables)
    smem = pl.BlockSpec(memory_space=pltpu.SMEM)
    result = pl.pallas_call(
        finish,
        out_shape=jax.ShapeDtypeStruct((8, 2, 128, 128), jnp.float32),
        in_specs=[smem, smem, vmem],
        out_specs=any_space,
        scratch_shapes=[pltpu.VMEM((8, 2, 128, 128), jnp.float32), pltpu.SemaphoreType.DMA((8,))],
        compiler_params=pltpu.CompilerParams(vmem_limit_bytes=60 * 1024 * 1024),
    )(listed, counted, back)
    return result[None, None]


def solution(mesh):
    in_specs = (
        P("depth", "tile", None, None, None, None),
        P(),
        P("depth", None, "tile", None),
        P(None, "tile", None, None),
        P(None, "tile"),
    )
    out_specs = P("depth", "tile", None, None, None, None)
    return jax.shard_map(
        per_device, mesh=mesh, in_specs=in_specs, out_specs=out_specs, check_vma=False
    )
```

```python
import functools
import math

import jax
import jax.numpy as jnp
import ml_dtypes
import numpy as np
from jax import lax
from jax.experimental import pallas as pl
from jax.experimental.pallas import tpu as pltpu
from jax.sharding import PartitionSpec as P

STEPS = 4
FRESNEL_RATE = 0.3
MESH = pl.DeviceIdType.MESH

ROWS = 272
TOP = 32766.0


def split_table(table):
    high = table.astype(ml_dtypes.bfloat16)
    low = (table - high.astype(np.float64)).astype(ml_dtypes.bfloat16)
    return high, low


def propagator(width):
    index = np.arange(width)
    angle = 2.0 * math.pi / width * ((index[:, None] * index[None, :]) % width)
    forward = np.cos(angle) - 1j * np.sin(angle)
    inverse = (np.cos(angle) + 1j * np.sin(angle)) / width
    freq = np.where(index < width // 2, index, index - width).astype(np.float64)
    phase = -2.0 * math.pi * FRESNEL_RATE / width * freq**2
    matrix = inverse @ ((np.cos(phase) + 1j * np.sin(phase))[:, None] * forward)
    real, imag = matrix.real, matrix.imag
    right = np.block([[real, imag], [-imag, real]])
    left = np.block([[real, -imag], [imag, real]])
    return split_table(right) + split_table(left)


def offset_of(slot):
    pair = slot // 2
    return lax.rem(16 + (lax.rem(pair, 2) * 2 - 1) * ((pair + 1) // 2) + 4 * lax.rem(slot, 2), 8)


def slot_of(offset):
    side = jnp.where((offset >= 3) & (offset <= 6), 1, 0)
    base = (offset + 4 * side) % 8
    return 2 * jnp.where(base == 7, 2, jnp.where(base == 2, 3, base)) + side


def encode(plane):
    groups = plane.reshape(16, 8, 128)
    largest = jnp.maximum(jnp.max(jnp.abs(groups), axis=0), 1e-30)
    power = jnp.ceil(jnp.log2(largest) * 256.0)
    scale = jnp.exp2(power * (-1.0 / 256.0)) * TOP
    coded = jnp.round(groups * scale[None]).reshape(128, 128)
    return coded.astype(jnp.int32).astype(jnp.int16), power


def store_wave(ref, real, imag):
    coded_real, power_real = encode(real)
    coded_imag, power_imag = encode(imag)
    ref[0:128, :] = coded_real
    ref[128:256, :] = coded_imag
    powers = jnp.concatenate([power_real, power_imag], axis=0)
    ref[256:272, :] = powers.astype(jnp.int32).astype(jnp.int16)


def decode(coded):
    numbers = coded.astype(jnp.int32).astype(jnp.float32)
    scales = jnp.exp2(numbers[256:272] * (1.0 / 256.0)) * (1.0 / TOP)
    real = (numbers[0:128].reshape(16, 8, 128) * scales[0:8][None]).reshape(128, 128)
    imag = (numbers[128:256].reshape(16, 8, 128) * scales[8:16][None]).reshape(128, 128)
    return real, imag


def split(value):
    high = value.astype(jnp.bfloat16)
    return high, (value - high.astype(jnp.float32)).astype(jnp.bfloat16)


def dot(a, b):
    return jnp.dot(a, b, preferred_element_type=jnp.float32)


def kernel(
    listed, counts, fronts, probe, obj, tables, back,
    listed_s, counts_s, listed_v, counts_v, tables_v, fronts_v, probe_v, obj_b, obj_f,
    lists, lists_v, lists_s, send0, waves, made,
    local_sem, list_send, list_recv, in_send, in_recv, hop_send, hop_recv, out_send, out_recv,
):
    d = lax.axis_index("depth")
    u = lax.axis_index("tile")
    n_depth = lax.axis_size("depth")
    batches = listed.shape[-1]

    barrier = pltpu.get_barrier_semaphore()
    for j in range(1, 8):
        pl.semaphore_signal(barrier, inc=1, device_id=(d, lax.rem(u + j, 8)), device_id_type=MESH)
    pl.semaphore_signal(barrier, inc=1, device_id=(lax.rem(d + 1, n_depth), u), device_id_type=MESH)
    pl.semaphore_signal(barrier, inc=1, device_id=(lax.rem(d + n_depth - 1, n_depth), u), device_id_type=MESH)

    pairs = ((listed, listed_v), (counts, counts_v), (listed, listed_s), (counts, counts_s), (fronts, fronts_v),
             (probe, probe_v), (obj, obj_b), (tables, tables_v))
    gets = [pltpu.make_async_copy(a, b, local_sem.at[i]) for i, (a, b) in enumerate(pairs)]
    for get in gets:
        get.start()

    first = n_depth - 1 - d
    gets[0].wait()
    gets[1].wait()
    probes = lax.broadcasted_iota(jnp.int32, (8, batches), 0)
    live = probes < counts_v[...]
    slots = jnp.where(live, slot_of(lax.rem(u - listed_v[0] + 8, 8)), -1)
    for j in range(8):
        chosen = slots == j
        for field in range(2):
            lists[j, field:field + 1, :] = jnp.sum(
                jnp.where(chosen, listed_v[1 + field], 0), axis=0, keepdims=True)

    for get in gets[2:5]:
        get.wait()

    @pl.loop(0, 8)
    def _(j):
        target = lax.rem(u + 8 - offset_of(j), 8)
        count = counts_s[0, first]
        source = jnp.int32(0)
        for p in range(8):
            source = jnp.where((listed_s[0, p, first] == target) & (p < count), p, source)
        wave = fronts_v[source]

        @pl.when(j == 0)
        def _():
            store_wave(waves.at[0, 0], wave[0], wave[1])

        @pl.when(j > 0)
        def _():
            store_wave(send0.at[j], wave[0], wave[1])

    gets[5].wait()

    @pl.when(d == 0)
    def _():
        @pl.loop(0, 8)
        def _(j):
            for s in range(1, STEPS):
                store_wave(waves.at[s, j], probe_v[0], probe_v[1])

    pl.semaphore_wait(barrier, 9)

    def list_copy(j):
        return pltpu.make_async_remote_copy(
            lists.at[j], lists_v.at[j], list_send.at[j], list_recv.at[j],
            device_id=(d, lax.rem(u + 8 - offset_of(j), 8)), device_id_type=MESH)

    def in_copy(j):
        return pltpu.make_async_remote_copy(
            send0.at[j], waves.at[0, j], in_send.at[j], in_recv.at[j],
            device_id=(d, lax.rem(u + 8 - offset_of(j), 8)), device_id_type=MESH)

    def hop_copy(s, pair):
        return pltpu.make_async_remote_copy(
            made.at[s, pl.ds(2 * pair, 2)], waves.at[s + 1, pl.ds(2 * pair, 2)],
            hop_send.at[s, pair], hop_recv.at[s, pair],
            device_id=(lax.rem(d + 1, n_depth), u), device_id_type=MESH)

    def out_copy(j):
        return pltpu.make_async_remote_copy(
            made.at[3, j], back.at[j], out_send.at[j], out_recv.at[j],
            device_id=(d, lax.rem(u + offset_of(j), 8)), device_id_type=MESH)

    @pl.loop(1, 8)
    def _(j):
        list_copy(j).start()

    @pl.loop(1, 8)
    def _(j):
        in_copy(j).start()

    lists_v[0] = lists[0]

    gets[6].wait()
    for layer in range(2):
        for part in range(2):
            for third in range(3):
                obj_f[layer, part, third] = obj_b[layer, part, :, third * 128:(third + 1) * 128].astype(jnp.float32)

    @pl.loop(1, 8)
    def _(j):
        list_copy(j).wait()

    get_lists = pltpu.make_async_copy(lists_v, lists_s, local_sem.at[8])
    get_lists.start()
    get_lists.wait()
    gets[7].wait()

    keep = pltpu.make_async_copy(made.at[3, 0], back.at[0], local_sem.at[9])
    lane = lax.broadcasted_iota(jnp.int32, (128, 128), 1)

    def cut(layer, part, row, column):
        third = lax.shift_right_logical(column, 7)
        left = lax.bitwise_and(column, 127)
        first = obj_f[layer, part, third, pl.ds(row, 128), :]
        second = obj_f[layer, part, jnp.minimum(third + 1, 2), pl.ds(row, 128), :]
        mixed = jnp.where(lane >= left, first, second)
        return pltpu.roll(mixed, lax.bitwise_and(128 - left, 127), 1)

    def one_task(s, pair):
        @pl.when(s == 0)
        def _():
            @pl.when(pair > 0)
            def _():
                in_copy(2 * pair).wait_recv()

            in_copy(2 * pair + 1).wait_recv()

        @pl.when((s > 0) & (d > 0))
        def _():
            hop_copy(s - 1, pair).wait_recv()

        real = [None, None]
        imag = [None, None]
        for side in range(2):
            real[side], imag[side] = decode(waves[s, 2 * pair + side])
        for layer in range(2):
            for side in range(2):
                row = lists_s[2 * pair + side, 0, first + s]
                column = lists_s[2 * pair + side, 1, first + s]
                trans_real = cut(layer, 0, row, column)
                trans_imag = cut(layer, 1, row, column)
                real[side], imag[side] = (
                    real[side] * trans_real - imag[side] * trans_imag,
                    real[side] * trans_imag + imag[side] * trans_real,
                )
            got = []
            for side in range(2):
                high, low = split(jnp.concatenate([real[side], imag[side]], axis=1))
                got.append(dot(high, tables_v[0]) + dot(high, tables_v[1]) + dot(low, tables_v[0]))
            high, low = split(jnp.concatenate([
                jnp.concatenate([got[0][:, 0:128], got[1][:, 0:128]], axis=1),
                jnp.concatenate([got[0][:, 128:256], got[1][:, 128:256]], axis=1),
            ], axis=0))
            got = [
                dot(tables_v[2, rows], high) + dot(tables_v[3, rows], high) + dot(tables_v[2, rows], low)
                for rows in (pl.ds(0, 128), pl.ds(128, 128))
            ]
            for side in range(2):
                real[side] = got[0][:, side * 128:(side + 1) * 128]
                imag[side] = got[1][:, side * 128:(side + 1) * 128]
        for side in range(2):
            store_wave(made.at[s, 2 * pair + side], real[side], imag[side])

        @pl.when((s < 3) & (d < n_depth - 1))
        def _():
            hop_copy(s, pair).start()

        @pl.when(s == 3)
        def _():
            @pl.when(pair > 0)
            def _():
                out_copy(2 * pair).start()

            @pl.when(pair == 0)
            def _():
                keep.start()

            out_copy(2 * pair + 1).start()

    @pl.loop(0, 7)
    def _(g):
        @pl.loop(0, 4)
        def _(i):
            s = i
            pair = g - s

            @pl.when((pair >= 0) & (pair < 4))
            def _():
                one_task(s, pair)

    @pl.loop(1, 8)
    def _(j):
        in_copy(j).wait_send()
        out_copy(j).wait()

    keep.wait()

    @pl.when(d < n_depth - 1)
    def _():
        @pl.loop(0, 3)
        def _(s):
            @pl.loop(0, 4)
            def _(pair):
                hop_copy(s, pair).wait_send()


def finish(listed_s, counts_s, back, out, out_v, sem):
    u = lax.axis_index("tile")
    last = lax.axis_size("depth") - 1 - lax.axis_index("depth") + STEPS - 1

    def put(p):
        return pltpu.make_async_copy(out_v.at[p], out.at[p], sem.at[p])

    @pl.loop(0, 8)
    def _(p):
        real, imag = decode(back[slot_of(lax.bitwise_and(u - listed_s[0, p, last], 7))])
        live = p < counts_s[0, last]
        out_v[p, 0] = jnp.where(live, real, 0.0)
        out_v[p, 1] = jnp.where(live, imag, 0.0)
        put(p).start()

    @pl.loop(0, 8)
    def _(p):
        put(p).wait()


def per_device(fronts, probe_wave, object_slices, patch_list, counts):
    tables = jnp.asarray(np.stack(propagator(128)))
    batches = counts.shape[0]
    any_space = pl.BlockSpec(memory_space=pl.ANY)
    vmem = pl.BlockSpec(memory_space=pltpu.VMEM)
    listed = jnp.transpose(patch_list[:, 0], (1, 2, 0))
    counted = jnp.transpose(counts)
    back = pl.pallas_call(
        kernel,
        out_shape=jax.ShapeDtypeStruct((8, ROWS, 128), jnp.int16),
        in_specs=[any_space] * 6,
        out_specs=any_space,
        scratch_shapes=[
            pltpu.SMEM((3, 8, batches), jnp.int32),
            pltpu.SMEM((1, batches), jnp.int32),
            pltpu.VMEM((3, 8, batches), jnp.int32),
            pltpu.VMEM((1, batches), jnp.int32),
            pltpu.VMEM((4, 256, 256), jnp.bfloat16),
            pltpu.VMEM((8, 2, 128, 128), jnp.float32),
            pltpu.VMEM((2, 128, 128), jnp.float32),
            pltpu.VMEM((2, 2, 384, 384), jnp.bfloat16),
            pltpu.VMEM((2, 2, 3, 384, 128), jnp.float32),
            pltpu.VMEM((8, 8, batches), jnp.int32),
            pltpu.VMEM((8, 8, batches), jnp.int32),
            pltpu.SMEM((8, 8, batches), jnp.int32),
            pltpu.VMEM((8, ROWS, 128), jnp.int16),
            pltpu.VMEM((STEPS, 8, ROWS, 128), jnp.int16),
            pltpu.VMEM((STEPS, 8, ROWS, 128), jnp.int16),
            pltpu.SemaphoreType.DMA((10,)),
            pltpu.SemaphoreType.DMA((8,)),
            pltpu.SemaphoreType.DMA((8,)),
            pltpu.SemaphoreType.DMA((8,)),
            pltpu.SemaphoreType.DMA((8,)),
            pltpu.SemaphoreType.DMA((3, 4)),
            pltpu.SemaphoreType.DMA((3, 4)),
            pltpu.SemaphoreType.DMA((8,)),
            pltpu.SemaphoreType.DMA((8,)),
        ],
        compiler_params=pltpu.CompilerParams(
            collective_id=0, has_side_effects=True, vmem_limit_bytes=60 * 1024 * 1024
        ),
    )(listed, counted, fronts[0, 0], probe_wave, object_slices, tables)
    smem = pl.BlockSpec(memory_space=pltpu.SMEM)
    result = pl.pallas_call(
        finish,
        out_shape=jax.ShapeDtypeStruct((8, 2, 128, 128), jnp.float32),
        in_specs=[smem, smem, vmem],
        out_specs=any_space,
        scratch_shapes=[pltpu.VMEM((8, 2, 128, 128), jnp.float32), pltpu.SemaphoreType.DMA((8,))],
        compiler_params=pltpu.CompilerParams(vmem_limit_bytes=60 * 1024 * 1024),
    )(listed, counted, back)
    return result[None, None]


def solution(mesh):
    in_specs = (
        P("depth", "tile", None, None, None, None),
        P(),
        P("depth", None, "tile", None),
        P(None, "tile", None, None),
        P(None, "tile"),
    )
    out_specs = P("depth", "tile", None, None, None, None)
    return jax.shard_map(
        per_device, mesh=mesh, in_specs=in_specs, out_specs=out_specs, check_vma=False
    )
```
